32 devices in a mesh: expert: 16 (over z, y, x), dp: 2 (over core).
Axes of the slice: x: 2, y: 2, z: 4, core: 2. Of those that a mesh axis runs over, the one named last changes fastest.
Arguments:
- tokens: bfloat16 [4096, 2048], P(('expert', 'dp')), may hold values from -6 to 6
- out_grad: bfloat16 [4096, 2048], P(('expert', 'dp')), may hold values from -6 to 6
- expert_ids: int32 [4096, 8], P(('expert', 'dp')), may hold values from 0 to 15, all different within a row; in each aligned block of 128 rows (0 to 127, 128 to 255, ...) at most 72 rows name the same one
- route_scores: float32 [4096, 8], P(('expert', 'dp')), may hold values from 0.05 to 1
- old_slot: int32 [16], replicated, may hold values from 0 to 15, as said below
- new_slot: int32 [16], replicated, may hold values from 0 to 15, as said below
- gate_up: bfloat16 [16, 2048, 768], P('expert'), may hold values from -0.125 to 0.125
- down: bfloat16 [16, 384, 2048], P('expert'), may hold values from -0.3125 to 0.3125
- first_gu: bfloat16 [16, 2048, 768], P('expert', 'dp'), may hold values from -12 to 12
- second_gu: bfloat16 [16, 2048, 768], P('expert', 'dp'), may hold values from 4 to 64
- first_down: bfloat16 [16, 384, 2048], P('expert', None, 'dp'), may hold values from -6 to 6
- second_down: bfloat16 [16, 384, 2048], P('expert', None, 'dp'), may hold values from 1 to 16
Outputs:
- mixed: bfloat16 [4096, 2048], P(('expert', 'dp'))
- token_grad: bfloat16 [4096, 2048], P(('expert', 'dp'))
- update_gu: bfloat16 [16, 2048, 768], P('expert', 'dp')
- update_down: bfloat16 [16, 384, 2048], P('expert', None, 'dp')
The draws below stay inside these ranges and needn't reach their ends.
Inputs may be any that keep to these rules, and one draw needn't show every extreme that they name: `expert_ids`: each row names 8 different experts; among the rows of one device no expert is named more than 72 times. `old_slot`: A permutation of the slots. `new_slot`: A permutation of the slots; it differs from old_slot in exactly 8 experts.
All inputs are finite; a program needn't handle non-finite values.
Results may differ from the reference program's by a relative error of at most 0.012.
Values may be sent and summed in bfloat16 or wider, within the bound.
A program may use at most 192 MiB of HBM per device.

```python
import math
import jax
import jax.numpy as jnp
import numpy as np
from jax import lax

D = 2048
TOP = 8
FF = 384
HOT = 8
TOK_DEV = 128
EXPERTS = 16
CAP = 72
TOKENS = 4096
N_EXPERT = 16
N_DP = 2


def placement_pair(key):
    order = jax.random.permutation(key, EXPERTS).astype(jnp.int32)
    movers = jax.random.permutation(jax.random.fold_in(key, 11), EXPERTS)[:HOT].astype(jnp.int32)
    shifted = jnp.roll(movers, -1)
    moved = order.at[movers].set(order[shifted])
    return (order, moved)


def draw_old_slot(key, part):
    shared = placement_pair(key)
    return shared[0]


def draw_new_slot(key, part):
    shared = placement_pair(key)
    return shared[1]


def shard_levels(stream_key, shape, shards, least, high):
    def one(axis_at, shards_of):
        steps = jax.random.uniform(jax.random.fold_in(jax.random.fold_in(stream_key, 6), axis_at), (shards_of,), jnp.float32, least / len(shards), high / len(shards))
        return jnp.repeat(jnp.exp(steps), shape[axis_at] // shards_of).reshape((-1,) + (1,) * (len(shape) - axis_at - 1))

    gain = one(*shards[0])
    for cut in shards[1:]:
        gain = gain * one(*cut)
    return gain


def assign_block(rng, own, number, rows, amount, top, most, slope):
    sequence = jax.random.permutation(rng, amount)
    crowded, usual = shares(amount, rows * top, most, slope, True), shares(amount, rows * top, most, slope, False)
    places = jnp.arange(amount)

    def named(lengths, rotation):
        used = int((lengths > 0).sum())
        fixed = max(1, used // 4)
        moved = fixed + (places - fixed + rotation * (used - fixed)) % max(1, amount - fixed)
        return jnp.zeros((amount,), jnp.int32).at[sequence[jnp.where(places < fixed, places, moved)]].set(jnp.asarray(lengths, jnp.int32))

    lengths = jnp.where(number % 4 == 0, named(crowded, number // 4), named(usual, number - number // 4 - 1))
    mixed = jax.random.permutation(jax.random.fold_in(own, 3), amount)
    giver, taker = mixed[0:amount // 2 * 2:2], mixed[1:amount // 2 * 2:2]
    slack = jnp.minimum(lengths[giver] - 1, most - lengths[taker]) // 2
    slack = jnp.where((giver == sequence[0]) | (taker == sequence[0]) | (lengths[taker] == 0), 0, jnp.maximum(slack, 0))
    moved = jax.random.randint(jax.random.fold_in(own, 4), (amount // 2,), 0, 1 << 20) % (slack + 1)
    lengths = lengths.at[giver].add(-moved).at[taker].add(moved)
    members = jnp.searchsorted(jnp.cumsum(lengths), jnp.arange(rows * top), side="right").astype(jnp.int32)
    listing = members.reshape(top, rows).T
    listing = listing[jax.random.permutation(jax.random.fold_in(own, 1), rows)]
    rotation = jax.random.randint(jax.random.fold_in(own, 2), (rows, 1), 0, top)
    return jnp.take_along_axis(listing, (jnp.arange(top)[None, :] + rotation) % top, axis=1)


def shares(amount, total, most, skew, full):
    weights = [(1 << 20) // math.isqrt(standing ** skew) + 1 for standing in range(1, amount + 1)]
    largest = most if full else min(most, max(-(-total // amount), total * weights[0] // sum(weights)))
    least = 1 if total - largest >= amount - 1 else 0
    holding, spare = [largest] + [least] * (amount - 1), total - largest - least * (amount - 1)
    while spare > 0:
        movable = [i for i in range(1, amount) if holding[i] < largest] or [i for i in range(1, amount) if holding[i] < most]
        mass, left = sum([weights[i] for i in movable]), spare
        for i in movable:
            extra = min(most - holding[i], max(1, left * weights[i] // mass), spare)
            holding[i] = holding[i] + extra
            spare = spare - extra
    return np.array(holding)


def normal_values(key, shape, spread, reach, cuts=(), kind=jnp.bfloat16):
    level = shard_levels(key, shape, cuts, -0.22, 0.18) if cuts else 1.0
    array = jax.random.normal(key, shape, jnp.float32) * spread * level
    return jnp.minimum(jnp.maximum(array, -reach), reach).astype(kind)


def setup_inputs(seed: int = 0) -> dict:
    arg_keys = jax.random.split(jax.random.key(seed), 13)
    tokens = normal_values(arg_keys[0], (TOKENS, D), 1.0, 6.0, ((0, 32),))
    out_grad = normal_values(arg_keys[1], (TOKENS, D), 1.0, 6.0, ((0, 32),))
    expert_ids_keys = jax.random.split(jax.random.fold_in(arg_keys[2], 1), TOKENS // TOK_DEV)
    expert_ids_turns = jax.random.permutation(jax.random.fold_in(arg_keys[2], 3), TOKENS // TOK_DEV)
    expert_ids = jax.vmap(lambda own, number: assign_block(jax.random.fold_in(arg_keys[2], 2), own, number, TOK_DEV, EXPERTS, TOP, CAP, 2))(expert_ids_keys, expert_ids_turns).reshape((TOKENS, TOP))
    route_scores = jnp.clip(jnp.exp(math.log(1.0) - 2.9957323 * jax.random.uniform(arg_keys[3], (TOKENS, TOP), jnp.float32) ** shard_levels(arg_keys[3], (TOKENS, TOP), ((0, 32),), -0.2, 0.2)), 0.05, 1.0)
    old_slot = draw_old_slot(jax.random.fold_in(arg_keys[12], 71), 0)
    new_slot = draw_new_slot(jax.random.fold_in(arg_keys[12], 71), 0)
    gate_up = normal_values(arg_keys[6], (EXPERTS, D, 2 * FF), D ** -0.5, 0.125, ((0, 16),))
    down = normal_values(arg_keys[7], (EXPERTS, FF, D), FF ** -0.5, 0.3125, ((0, 16),))
    first_gu = normal_values(arg_keys[8], (EXPERTS, D, 2 * FF), 3.0, 12.0, ((0, 16), (1, 2)))
    second_gu = jnp.clip(jnp.exp(math.log(64.0) - 2.7725887 * jax.random.uniform(arg_keys[9], (EXPERTS, D, 2 * FF), jnp.float32) ** shard_levels(arg_keys[9], (EXPERTS, D, 2 * FF), ((0, 16), (1, 2)), -0.2, 0.2)), 4.0, 64.0).astype(jnp.bfloat16)
    first_down = normal_values(arg_keys[10], (EXPERTS, FF, D), 1.5, 6.0, ((0, 16), (2, 2)))
    second_down = jnp.clip(jnp.exp(math.log(16.0) - 2.7725887 * jax.random.uniform(arg_keys[11], (EXPERTS, FF, D), jnp.float32) ** shard_levels(arg_keys[11], (EXPERTS, FF, D), ((0, 16), (2, 2)), -0.2, 0.2)), 1.0, 16.0).astype(jnp.bfloat16)
    return {"tokens": tokens, "out_grad": out_grad, "expert_ids": expert_ids, "route_scores": route_scores, "old_slot": old_slot, "new_slot": new_slot, "gate_up": gate_up, "down": down, "first_gu": first_gu, "second_gu": second_gu, "first_down": first_down, "second_down": second_down}


beta_one = 0.9
beta_two = 0.95
epsilon = 1e-08

def expert_forward(rows_x, w_gu, w_down):
    hidden = w_down.shape[0]
    both = jnp.dot(rows_x, w_gu, preferred_element_type=jnp.float32)
    gate = both[:, :hidden]
    upper = both[:, hidden:]
    activated = (gate * jax.nn.sigmoid(gate) * upper).astype(jnp.bfloat16)
    output = jnp.dot(activated, w_down, preferred_element_type=jnp.float32).astype(jnp.bfloat16)
    return (both, activated, output)

def expert_backward(rows_x, rows_cot, both, activated, w_gu, w_down):
    hidden = w_down.shape[0]
    gate = both[:, :hidden]
    upper = both[:, hidden:]
    sigmoid_gate = jax.nn.sigmoid(gate)
    grad_act = lax.dot_general(rows_cot, w_down, (((1,), (1,)), ((), ())), preferred_element_type=jnp.float32)
    grad_gate = grad_act * upper * (sigmoid_gate * (1.0 + gate * (1.0 - sigmoid_gate)))
    grad_upper = grad_act * gate * sigmoid_gate
    grad_both = jnp.concatenate([grad_gate, grad_upper], axis=1).astype(jnp.bfloat16)
    row_grad = lax.dot_general(grad_both, w_gu, (((1,), (1,)), ((), ())), preferred_element_type=jnp.float32).astype(jnp.bfloat16)
    grad_gu = lax.dot_general(rows_x, grad_both, (((0,), (0,)), ((), ())), preferred_element_type=jnp.float32)
    grad_down = lax.dot_general(activated, rows_cot, (((0,), (0,)), ((), ())), preferred_element_type=jnp.float32)
    return (row_grad, grad_gu, grad_down)

def adam_direction(first, second, grad):
    first_new = beta_one * first.astype(jnp.float32) + (1.0 - beta_one) * grad
    second_new = beta_two * second.astype(jnp.float32) + (1.0 - beta_two) * grad * grad
    first_fix = 1.0 - beta_one ** 10.0
    second_fix = 1.0 - beta_two ** 10.0
    return (first_new / first_fix / (jnp.sqrt(second_new / second_fix) + epsilon)).astype(jnp.bfloat16)

def reference(tokens, out_grad, expert_ids, route_scores, old_slot, new_slot, gate_up, down, first_gu, second_gu, first_down, second_down):
    probs = route_scores / lax.optimization_barrier(jnp.sum(route_scores, axis=1, keepdims=True))
    span = N_EXPERT * CAP
    per_group = N_EXPERT * TOK_DEV
    assigned = per_group * TOP
    grid_tokens = tokens.reshape(N_EXPERT, N_DP, TOK_DEV, D)
    grid_grad = out_grad.reshape(N_EXPERT, N_DP, TOK_DEV, D)
    grid_ids = expert_ids.reshape(N_EXPERT, N_DP, TOK_DEV, TOP)
    grid_probs = probs.reshape(N_EXPERT, N_DP, TOK_DEV, TOP)
    columns = jnp.arange(EXPERTS, dtype=jnp.int32)
    mixed_parts = []
    grad_parts = []
    total_gu = jnp.zeros((EXPERTS, D, 2 * FF), jnp.float32)
    total_down = jnp.zeros((EXPERTS, FF, D), jnp.float32)
    for side in range(N_DP):
        rows_x = jnp.concatenate([grid_tokens[:, side].reshape(per_group, D), jnp.zeros((1, D), jnp.bfloat16)], axis=0)
        rows_dy = jnp.concatenate([grid_grad[:, side].reshape(per_group, D), jnp.zeros((1, D), jnp.bfloat16)], axis=0)
        flat_ids = grid_ids[:, side].reshape(assigned)
        group_probs = grid_probs[:, side].reshape(per_group, TOP)
        flat_probs = jnp.concatenate([group_probs.reshape(assigned), jnp.zeros((1,), jnp.float32)], axis=0)
        onehot = (flat_ids[:, None] == columns[None, :]).astype(jnp.int32)
        place = lax.optimization_barrier(jnp.sum(onehot * (jnp.cumsum(onehot, axis=0) - 1), axis=1))
        where_flat = (flat_ids * span + place).astype(jnp.int32)
        table = jnp.full((EXPERTS * span,), assigned, jnp.int32)
        table = table.at[where_flat].set(jnp.arange(assigned, dtype=jnp.int32)).reshape(EXPERTS, span)

        def one_expert(expert):
            index = table[expert]
            token = index // TOP
            picked_x = rows_x[token]
            picked_cot = (flat_probs[index][:, None] * rows_dy[token].astype(jnp.float32)).astype(jnp.bfloat16)
            source = old_slot[expert]
            w_gu = gate_up[source]
            w_down = down[source]
            both, activated, output = expert_forward(picked_x, w_gu, w_down)
            row_grad, grad_gu, grad_down = expert_backward(picked_x, picked_cot, both, activated, w_gu, w_down)
            return (output, row_grad, grad_gu.astype(jnp.bfloat16), grad_down.astype(jnp.bfloat16))
        outputs, row_grads, part_gu, part_down = lax.map(one_expert, columns)
        got_out = outputs.reshape(EXPERTS * span, D)[where_flat].reshape(per_group, TOP, D)
        got_grad = row_grads.reshape(EXPERTS * span, D)[where_flat].reshape(per_group, TOP, D)
        mixed_side = lax.optimization_barrier(jnp.sum(group_probs[:, :, None] * got_out.astype(jnp.float32), axis=1)).astype(jnp.bfloat16)
        grad_side = lax.optimization_barrier(jnp.sum(got_grad.astype(jnp.float32), axis=1)).astype(jnp.bfloat16)
        mixed_parts.append(mixed_side.reshape(N_EXPERT, TOK_DEV, D))
        grad_parts.append(grad_side.reshape(N_EXPERT, TOK_DEV, D))
        total_gu = total_gu + part_gu.astype(jnp.float32)
        total_down = total_down + part_down.astype(jnp.float32)
    mixed = jnp.stack(mixed_parts, axis=1).reshape(TOKENS, D)
    token_grad = jnp.stack(grad_parts, axis=1).reshape(TOKENS, D)
    step_gu = adam_direction(jnp.take(first_gu, old_slot, axis=0), jnp.take(second_gu, old_slot, axis=0), total_gu)
    step_down = adam_direction(jnp.take(first_down, old_slot, axis=0), jnp.take(second_down, old_slot, axis=0), total_down)
    update_gu = jnp.zeros((EXPERTS, D, 2 * FF), jnp.bfloat16).at[new_slot].set(step_gu)
    update_down = jnp.zeros((EXPERTS, FF, D), jnp.bfloat16).at[new_slot].set(step_down)
    return (mixed, token_grad, update_gu, update_down)
```

```python
import jax
import jax.numpy as jnp
from jax import lax
from jax.sharding import PartitionSpec as P

beta_one = 0.9
beta_two = 0.95
epsilon = 1e-08


def expert_forward(rows_x, w_gu, w_down):
    hidden = w_down.shape[0]
    both = jnp.dot(rows_x, w_gu, preferred_element_type=jnp.float32)
    gate = both[:, :hidden]
    upper = both[:, hidden:]
    activated = (gate * jax.nn.sigmoid(gate) * upper).astype(jnp.bfloat16)
    output = jnp.dot(activated, w_down, preferred_element_type=jnp.float32).astype(jnp.bfloat16)
    return (both, activated, output)


def expert_backward(rows_x, rows_cot, both, activated, w_gu, w_down):
    hidden = w_down.shape[0]
    gate = both[:, :hidden]
    upper = both[:, hidden:]
    sigmoid_gate = jax.nn.sigmoid(gate)
    grad_act = lax.dot_general(
        rows_cot, w_down, (((1,), (1,)), ((), ())), preferred_element_type=jnp.float32
    )
    grad_gate = grad_act * upper * (sigmoid_gate * (1.0 + gate * (1.0 - sigmoid_gate)))
    grad_upper = grad_act * gate * sigmoid_gate
    grad_both = jnp.concatenate([grad_gate, grad_upper], axis=1).astype(jnp.bfloat16)
    row_grad = lax.dot_general(
        grad_both, w_gu, (((1,), (1,)), ((), ())), preferred_element_type=jnp.float32
    ).astype(jnp.bfloat16)
    grad_gu = lax.dot_general(
        rows_x, grad_both, (((0,), (0,)), ((), ())), preferred_element_type=jnp.float32
    )
    grad_down = lax.dot_general(
        activated, rows_cot, (((0,), (0,)), ((), ())), preferred_element_type=jnp.float32
    )
    return (row_grad, grad_gu, grad_down)


def adam_direction(first, second, grad):
    first_new = beta_one * first.astype(jnp.float32) + (1.0 - beta_one) * grad
    second_new = beta_two * second.astype(jnp.float32) + (1.0 - beta_two) * grad * grad
    first_fix = 1.0 - beta_one**10.0
    second_fix = 1.0 - beta_two**10.0
    return (first_new / first_fix / (jnp.sqrt(second_new / second_fix) + epsilon)).astype(
        jnp.bfloat16
    )


def spread(block, count):
    part = block.shape[0] // count
    return lax.all_to_all(
        block.reshape(count, part, block.shape[1]), "expert", split_axis=0, concat_axis=0, tiled=True
    )


def land(pieces, source):
    ordered = jnp.take(pieces, source, axis=0)
    back = lax.all_to_all(ordered, "expert", split_axis=0, concat_axis=0, tiled=True)
    return back.reshape(-1, back.shape[2])


def rows_by_exchange(tokens, out_grad, target, probs, w_gu, w_down):
    count = lax.axis_size("expert")
    tok_rows, width = tokens.shape
    top = target.shape[1]
    capacity = max(2, tok_rows * top * 9 // (8 * count))
    rows = count * capacity
    lanes = jnp.arange(count, dtype=jnp.int32)
    flat_target = target.reshape(-1)
    onehot = (flat_target[:, None] == lanes[None, :]).astype(jnp.int32)
    place = jnp.sum(onehot * (jnp.cumsum(onehot, axis=0) - 1), axis=1)
    slot = flat_target * capacity + place
    match = slot[None, :] == jnp.arange(rows, dtype=jnp.int32)[:, None]
    pick = jnp.any(match.reshape(rows, tok_rows, top), axis=2).astype(jnp.bfloat16)
    slot_prob = jnp.sum(jnp.where(match, probs.reshape(1, -1), 0.0), axis=1)
    send_x = (
        jnp.dot(pick, tokens, preferred_element_type=jnp.float32)
        .astype(jnp.bfloat16)
        .reshape(count, capacity, width)
    )
    send_cot = (
        (jnp.dot(pick, out_grad, preferred_element_type=jnp.float32) * slot_prob[:, None])
        .astype(jnp.bfloat16)
        .reshape(count, capacity, width)
    )
    recv_x = lax.all_to_all(send_x, "expert", split_axis=0, concat_axis=0, tiled=True)
    rows_x = recv_x.reshape(rows, width)
    both, activated, output = expert_forward(rows_x, w_gu, w_down)
    back_out = lax.all_to_all(
        output.reshape(count, capacity, width), "expert", split_axis=0, concat_axis=0, tiled=True
    )
    recv_cot = lax.all_to_all(send_cot, "expert", split_axis=0, concat_axis=0, tiled=True)
    rows_cot = recv_cot.reshape(rows, width)
    row_grad, grad_gu, grad_down = expert_backward(rows_x, rows_cot, both, activated, w_gu, w_down)
    back_grad = lax.all_to_all(
        row_grad.reshape(count, capacity, width), "expert", split_axis=0, concat_axis=0, tiled=True
    )
    back_pick = lambda weight, piece: lax.dot_general(
        weight.astype(jnp.bfloat16),
        piece.reshape(rows, width),
        (((0,), (0,)), ((), ())),
        preferred_element_type=jnp.float32,
    )
    weight = pick.astype(jnp.float32) * slot_prob[:, None]
    coarse = lax.reduce_precision(weight, 8, 7)
    mixed = (back_pick(coarse, back_out) + back_pick(weight - coarse, back_out)).astype(jnp.bfloat16)
    token_grad = back_pick(pick, back_grad).astype(jnp.bfloat16)
    return (mixed, token_grad, grad_gu, grad_down)


def per_device(
    tokens,
    out_grad,
    expert_ids,
    route_scores,
    old_slot,
    new_slot,
    gate_up,
    down,
    first_gu,
    second_gu,
    first_down,
    second_down,
):
    count = lax.axis_size("expert")
    lanes = jnp.arange(count, dtype=jnp.int32)
    owner = new_slot[None, :] == lanes[:, None]
    source = jnp.sum(jnp.where(owner, old_slot[None, :], 0), axis=1)
    probs = route_scores / jnp.sum(route_scores, axis=1, keepdims=True)
    target = jnp.sum(
        jnp.where(expert_ids[:, :, None] == lanes[None, None, :], old_slot[None, None, :], 0),
        axis=2,
    )
    mixed, token_grad, grad_gu, grad_down = rows_by_exchange(
        tokens, out_grad, target, probs, gate_up[0], down[0]
    )
    share_gu, share_down = (
        lax.psum_scatter(
            grad_gu.astype(jnp.bfloat16), "dp", scatter_dimension=0, tiled=True
        ).astype(jnp.float32),
        lax.psum_scatter(
            grad_down.astype(jnp.bfloat16), "dp", scatter_dimension=1, tiled=True
        ).astype(jnp.float32),
    )
    step_gu = adam_direction(first_gu[0], second_gu[0], share_gu)
    step_down = adam_direction(first_down[0], second_down[0], share_down)
    update_gu = land(spread(step_gu, count), source)[None]
    update_down = land(spread(step_down, count), source)[None]
    return (mixed, token_grad, update_gu, update_down)


def solution(mesh):
    placed = (
        P(("expert", "dp"), None),
        P(("expert", "dp"), None),
        P(("expert", "dp"), None),
        P(("expert", "dp"), None),
        P(),
        P(),
        P("expert", None, None),
        P("expert", None, None),
        P("expert", "dp", None),
        P("expert", "dp", None),
        P("expert", None, "dp"),
        P("expert", None, "dp"),
    )
    return jax.shard_map(
        per_device,
        mesh=mesh,
        in_specs=placed,
        out_specs=(
            P(("expert", "dp"), None),
            P(("expert", "dp"), None),
            P("expert", "dp", None),
            P("expert", None, "dp"),
        ),
        check_vma=False,
    )
```

```python
import functools

import jax
import jax.numpy as jnp
from jax import lax
from jax.experimental import pallas as pl
from jax.experimental.pallas import tpu as pltpu
from jax.sharding import PartitionSpec as P

MESH = pl.DeviceIdType.MESH
SIDE = 2
PLANE = SIDE * SIDE

beta_one = 0.9
beta_two = 0.95
epsilon = 1e-08


def expert_forward(rows_x, w_gu, w_down):
    hidden = w_down.shape[0]
    both = jnp.dot(rows_x, w_gu, preferred_element_type=jnp.float32)
    gate = both[:, :hidden]
    upper = both[:, hidden:]
    activated = (gate * jax.nn.sigmoid(gate) * upper).astype(jnp.bfloat16)
    output = jnp.dot(activated, w_down, preferred_element_type=jnp.float32).astype(jnp.bfloat16)
    return (both, activated, output)


def expert_backward(rows_x, rows_cot, both, activated, w_gu, w_down):
    hidden = w_down.shape[0]
    gate = both[:, :hidden]
    upper = both[:, hidden:]
    sigmoid_gate = jax.nn.sigmoid(gate)
    grad_act = lax.dot_general(
        rows_cot, w_down, (((1,), (1,)), ((), ())), preferred_element_type=jnp.float32
    )
    grad_gate = grad_act * upper * (sigmoid_gate * (1.0 + gate * (1.0 - sigmoid_gate)))
    grad_upper = grad_act * gate * sigmoid_gate
    grad_both = jnp.concatenate([grad_gate, grad_upper], axis=1).astype(jnp.bfloat16)
    row_grad = lax.dot_general(
        grad_both, w_gu, (((1,), (1,)), ((), ())), preferred_element_type=jnp.float32
    ).astype(jnp.bfloat16)
    grad_gu = lax.dot_general(
        rows_x, grad_both, (((0,), (0,)), ((), ())), preferred_element_type=jnp.float32
    )
    grad_down = lax.dot_general(
        activated, rows_cot, (((0,), (0,)), ((), ())), preferred_element_type=jnp.float32
    )
    return (row_grad, grad_gu, grad_down)


def adam_direction(first, second, grad):
    first_new = beta_one * first.astype(jnp.float32) + (1.0 - beta_one) * grad
    second_new = beta_two * second.astype(jnp.float32) + (1.0 - beta_two) * grad * grad
    first_fix = 1.0 - beta_one**10.0
    second_fix = 1.0 - beta_two**10.0
    return (first_new / first_fix / (jnp.sqrt(second_new / second_fix) + epsilon)).astype(
        jnp.bfloat16
    )


def spread(block, count):
    part = block.shape[0] // count
    return lax.all_to_all(
        block.reshape(count, part, block.shape[1]), "expert", split_axis=0, concat_axis=0, tiled=True
    )


def land(pieces, source):
    ordered = jnp.take(pieces, source, axis=0)
    back = lax.all_to_all(ordered, "expert", split_axis=0, concat_axis=0, tiled=True)
    return back.reshape(-1, back.shape[2])


def position(count):
    deep = count // PLANE
    me = lax.axis_index("expert")
    return (deep, me // PLANE, (me // SIDE) % SIDE, me % SIDE)


def slot_of(z, y, x):
    return z * PLANE + y * SIDE + x


def greet(partners):
    barrier = pltpu.get_barrier_semaphore()
    for partner in partners:
        pl.semaphore_signal(barrier, inc=1, device_id=partner, device_id_type=MESH)
    pl.semaphore_wait(barrier, len(partners))


def gather_kernel(count, *refs):
    tensors = 2
    sources, outs = refs[:tensors], refs[tensors : 2 * tensors]
    own_sem, z_send, z_recv, xy_send, xy_recv, d_send, d_recv = refs[2 * tensors :]
    deep, z, y, x = position(count)
    core = lax.axis_index("dp")
    half = sources[0].shape[0] // 2
    up = [(slot_of((z + k) % deep, y, x), core) for k in range(deep)]
    beside = ((slot_of(z, y, 1 - x), core), (slot_of(z, 1 - y, x), core))
    greet(up[1:] + list(beside))

    def copy(src, dst, send, recv, device):
        return pltpu.make_async_remote_copy(
            src_ref=src, dst_ref=dst, send_sem=send, recv_sem=recv,
            device_id=device, device_id_type=MESH,
        )

    def across(t, k, origin):
        return copy(sources[t], outs[t].at[origin], z_send.at[t, k - 1], z_recv.at[t, k - 1], up[k])

    def to_side(t, k, way, src, origin):
        return copy(
            src, outs[t].at[origin], xy_send.at[t, k, way], xy_recv.at[t, k, way], beside[way]
        )

    def onward(t, k, way, origin):
        rows = pl.ds(way * half, half)
        piece = outs[t].at[origin, rows]
        return copy(piece, piece, d_send.at[t, k, way], d_recv.at[t, k, way], beside[1 - way])

    me = slot_of(z, y, x)
    sent = []
    locals_ = []
    for t in range(tensors):
        own = pltpu.make_async_copy(sources[t], outs[t].at[me], own_sem.at[t])
        own.start()
        locals_.append(own)
    for t in range(tensors):
        for way in range(2):
            step = to_side(t, 0, way, sources[t], me)
            step.start()
            sent.append(step)
        for k in range(1, deep):
            step = across(t, k, me)
            step.start()
            sent.append(step)

    def forward(t, k):
        zk = (z - k + deep) % deep
        came = (slot_of(zk, y, 1 - x), slot_of(zk, 1 - y, x))
        for way in range(2):
            to_side(t, k, way, outs[t].at[came[way]], came[way]).wait_recv()
            step = onward(t, k, way, came[way])
            step.start()
            sent.append(step)

    for t in range(tensors):
        for k in range(1, deep):
            origin = slot_of((z - k + deep) % deep, y, x)
            across(t, k, origin).wait_recv()
            for way in range(2):
                step = to_side(t, k, way, outs[t].at[origin], origin)
                step.start()
                sent.append(step)
            forward(t, k - 1)
        forward(t, deep - 1)
    for t in range(tensors):
        for k in range(deep):
            zk = (z - k + deep) % deep
            for way in range(2):
                onward(t, k, way, slot_of(zk, 1 - y, 1 - x)).wait_recv()
    for own in locals_:
        own.wait()
    for step in sent:
        step.wait_send()


def gather_rows(tokens, out_grad):
    count = lax.axis_size("expert")
    rows, width = tokens.shape
    deep = count // PLANE
    dma = pltpu.SemaphoreType.DMA
    full = jax.ShapeDtypeStruct((count, rows, width), tokens.dtype)
    got = pl.pallas_call(
        functools.partial(gather_kernel, count),
        out_shape=(full, full),
        in_specs=[pl.BlockSpec(memory_space=pl.ANY)] * 2,
        out_specs=(pl.BlockSpec(memory_space=pl.ANY),) * 2,
        scratch_shapes=[
            dma((2,)),
            dma((2, deep - 1)),
            dma((2, deep - 1)),
            dma((2, deep, 2)),
            dma((2, deep, 2)),
            dma((2, deep, 2)),
            dma((2, deep, 2)),
        ],
        compiler_params=pltpu.CompilerParams(collective_id=0, has_side_effects=True),
    )(tokens, out_grad)
    return tuple(part.reshape(count * rows, width) for part in got)


def sum_kernel(count, *refs):
    tensors = 2
    parts, outs = refs[:tensors], refs[tensors : 2 * tensors]
    (got_d, got_xy, got_z, out_xy, out_z,
     z_send, z_recv, xy_send, xy_recv, d_send, d_recv) = refs[2 * tensors :]
    deep, z, y, x = position(count)
    core = lax.axis_index("dp")
    half = outs[0].shape[0] // 2
    up = [(slot_of((z + k) % deep, y, x), core) for k in range(deep)]
    beside = ((slot_of(z, y, 1 - x), core), (slot_of(z, 1 - y, x), core))
    greet(up[1:] + list(beside))

    def copy(src, dst, send, recv, device):
        return pltpu.make_async_remote_copy(
            src_ref=src, dst_ref=dst, send_sem=send, recv_sem=recv,
            device_id=device, device_id_type=MESH,
        )

    def wide(ref, index):
        return ref[index].astype(jnp.float32)

    order = [(k + 1) % deep for k in range(deep)]
    jobs = [(t, k) for t in range(tensors) for k in order]
    sent = []
    first = {}
    for t, k in jobs:
        far = slot_of((z + k) % deep, 1 - y, 1 - x)
        for way in range(2):
            step = copy(
                parts[t].at[far, pl.ds(way * half, half)], got_d.at[t, k, way],
                d_send.at[t, k, way], d_recv.at[t, k, way], beside[1 - way],
            )
            step.start()
            first[t, k, way] = step
            sent.append(step)
    second = {}

    def pass_on(t, k):
        zk = (z + k) % deep
        near = (slot_of(zk, y, 1 - x), slot_of(zk, 1 - y, x))
        for way in range(2):
            first[t, k, way].wait_recv()
            rows, rest = pl.ds(way * half, half), pl.ds((1 - way) * half, half)
            total = wide(parts[t], (near[way], rows)) + wide(got_d, (t, k, way))
            out_xy[t, k, way, rows] = total.astype(jnp.bfloat16)
            out_xy[t, k, way, rest] = parts[t][near[way], rest]
            step = copy(
                out_xy.at[t, k, way], got_xy.at[t, k, way],
                xy_send.at[t, k, way], xy_recv.at[t, k, way], beside[way],
            )
            step.start()
            second[t, k, way] = step
            sent.append(step)

    third = {}

    def plane_sum(t, k):
        second[t, k, 0].wait_recv()
        second[t, k, 1].wait_recv()
        total = wide(got_xy, (t, k, 0)) + wide(got_xy, (t, k, 1))
        return total + wide(parts[t], slot_of((z + k) % deep, y, x))

    def leave(t, k):
        if k == 0:
            return
        out_z[t, k - 1] = plane_sum(t, k).astype(jnp.bfloat16)
        step = copy(
            out_z.at[t, k - 1], got_z.at[t, k - 1], z_send.at[t, k - 1], z_recv.at[t, k - 1], up[k]
        )
        step.start()
        third[t, k] = step
        sent.append(step)

    pass_on(*jobs[0])
    for now, after in zip(jobs, jobs[1:]):
        pass_on(*after)
        leave(*now)
    for t in range(tensors):
        total = plane_sum(t, 0)
        for k in range(1, deep):
            third[t, k].wait_recv()
            total = total + wide(got_z, (t, k - 1))
        outs[t][...] = total.astype(jnp.bfloat16)
    for step in sent:
        step.wait_send()


def sum_rows(part_out, part_grad):
    count = lax.axis_size("expert")
    rows, width = part_out.shape[0] // count, part_out.shape[1]
    deep = count // PLANE
    dma = pltpu.SemaphoreType.DMA
    block = jax.ShapeDtypeStruct((rows, width), part_out.dtype)
    vmem = lambda *lead: pltpu.VMEM(lead + (width,), jnp.bfloat16)
    return pl.pallas_call(
        functools.partial(sum_kernel, count),
        out_shape=(block, block),
        in_specs=[pl.BlockSpec(memory_space=pltpu.VMEM)] * 2,
        out_specs=(pl.BlockSpec(memory_space=pltpu.VMEM),) * 2,
        scratch_shapes=[
            vmem(2, deep, 2, rows // 2),
            vmem(2, deep, 2, rows),
            vmem(2, deep - 1, rows),
            vmem(2, deep, 2, rows),
            vmem(2, deep - 1, rows),
            dma((2, deep - 1)),
            dma((2, deep - 1)),
            dma((2, deep, 2)),
            dma((2, deep, 2)),
            dma((2, deep, 2)),
            dma((2, deep, 2)),
        ],
        compiler_params=pltpu.CompilerParams(
            collective_id=1, has_side_effects=True, vmem_limit_bytes=56 * 1024 * 1024
        ),
    )(part_out.reshape(count, rows, width), part_grad.reshape(count, rows, width))


def rows_by_gather(tokens, out_grad, target, probs, w_gu, w_down):
    count = lax.axis_size("expert")
    lanes = jnp.arange(count, dtype=jnp.int32)
    chosen = target[:, :, None] == lanes[None, None, :]
    weights = jnp.sum(jnp.where(chosen, probs[:, :, None], 0.0), axis=1).T
    prob_in = lax.all_to_all(weights, "expert", split_axis=0, concat_axis=0, tiled=True)
    rows_x, rows_g = gather_rows(tokens, out_grad)
    prob = prob_in.reshape(-1, 1)
    both, activated, output = expert_forward(rows_x, w_gu, w_down)
    rows_cot = (prob * rows_g.astype(jnp.float32)).astype(jnp.bfloat16)
    row_grad, grad_gu, grad_down = expert_backward(rows_x, rows_cot, both, activated, w_gu, w_down)
    mixed, token_grad = sum_rows(
        (prob * output.astype(jnp.float32)).astype(jnp.bfloat16), row_grad
    )
    return (mixed, token_grad, grad_gu, grad_down)


def rows_by_exchange(tokens, out_grad, target, probs, w_gu, w_down):
    count = lax.axis_size("expert")
    tok_rows, width = tokens.shape
    top = target.shape[1]
    capacity = max(2, tok_rows * top * 9 // (8 * count))
    rows = count * capacity
    lanes = jnp.arange(count, dtype=jnp.int32)
    flat_target = target.reshape(-1)
    onehot = (flat_target[:, None] == lanes[None, :]).astype(jnp.int32)
    place = jnp.sum(onehot * (jnp.cumsum(onehot, axis=0) - 1), axis=1)
    slot = flat_target * capacity + place
    match = slot[None, :] == jnp.arange(rows, dtype=jnp.int32)[:, None]
    pick = jnp.any(match.reshape(rows, tok_rows, top), axis=2).astype(jnp.bfloat16)
    slot_prob = jnp.sum(jnp.where(match, probs.reshape(1, -1), 0.0), axis=1)
    send_x = (
        jnp.dot(pick, tokens, preferred_element_type=jnp.float32)
        .astype(jnp.bfloat16)
        .reshape(count, capacity, width)
    )
    send_cot = (
        (jnp.dot(pick, out_grad, preferred_element_type=jnp.float32) * slot_prob[:, None])
        .astype(jnp.bfloat16)
        .reshape(count, capacity, width)
    )
    recv_x = lax.all_to_all(send_x, "expert", split_axis=0, concat_axis=0, tiled=True)
    rows_x = recv_x.reshape(rows, width)
    both, activated, output = expert_forward(rows_x, w_gu, w_down)
    back_out = lax.all_to_all(
        output.reshape(count, capacity, width), "expert", split_axis=0, concat_axis=0, tiled=True
    )
    recv_cot = lax.all_to_all(send_cot, "expert", split_axis=0, concat_axis=0, tiled=True)
    rows_cot = recv_cot.reshape(rows, width)
    row_grad, grad_gu, grad_down = expert_backward(rows_x, rows_cot, both, activated, w_gu, w_down)
    back_grad = lax.all_to_all(
        row_grad.reshape(count, capacity, width), "expert", split_axis=0, concat_axis=0, tiled=True
    )
    back_pick = lambda weight, piece: lax.dot_general(
        weight.astype(jnp.bfloat16),
        piece.reshape(rows, width),
        (((0,), (0,)), ((), ())),
        preferred_element_type=jnp.float32,
    )
    weight = pick.astype(jnp.float32) * slot_prob[:, None]
    coarse = lax.reduce_precision(weight, 8, 7)
    mixed = (back_pick(coarse, back_out) + back_pick(weight - coarse, back_out)).astype(jnp.bfloat16)
    token_grad = back_pick(pick, back_grad).astype(jnp.bfloat16)
    return (mixed, token_grad, grad_gu, grad_down)


def per_device(
    tokens,
    out_grad,
    expert_ids,
    route_scores,
    old_slot,
    new_slot,
    gate_up,
    down,
    first_gu,
    second_gu,
    first_down,
    second_down,
):
    count = lax.axis_size("expert")
    lanes = jnp.arange(count, dtype=jnp.int32)
    owner = new_slot[None, :] == lanes[:, None]
    source = jnp.sum(jnp.where(owner, old_slot[None, :], 0), axis=1)
    probs = route_scores / jnp.sum(route_scores, axis=1, keepdims=True)
    target = jnp.sum(
        jnp.where(expert_ids[:, :, None] == lanes[None, None, :], old_slot[None, None, :], 0),
        axis=2,
    )
    gathered = count % (2 * PLANE) == 0 and 2 * expert_ids.shape[1] >= count
    rows_plan = rows_by_gather if gathered else rows_by_exchange
    mixed, token_grad, grad_gu, grad_down = rows_plan(
        tokens, out_grad, target, probs, gate_up[0], down[0]
    )
    share_gu, share_down = (
        lax.psum_scatter(
            grad_gu.astype(jnp.bfloat16), "dp", scatter_dimension=0, tiled=True
        ).astype(jnp.float32),
        lax.psum_scatter(
            grad_down.astype(jnp.bfloat16), "dp", scatter_dimension=1, tiled=True
        ).astype(jnp.float32),
    )
    step_gu = adam_direction(first_gu[0], second_gu[0], share_gu)
    step_down = adam_direction(first_down[0], second_down[0], share_down)
    update_gu = land(spread(step_gu, count), source)[None]
    update_down = land(spread(step_down, count), source)[None]
    return (mixed, token_grad, update_gu, update_down)


def solution(mesh):
    placed = (
        P(("expert", "dp"), None),
        P(("expert", "dp"), None),
        P(("expert", "dp"), None),
        P(("expert", "dp"), None),
        P(),
        P(),
        P("expert", None, None),
        P("expert", None, None),
        P("expert", "dp", None),
        P("expert", "dp", None),
        P("expert", None, "dp"),
        P("expert", None, "dp"),
    )
    return jax.shard_map(
        per_device,
        mesh=mesh,
        in_specs=placed,
        out_specs=(
            P(("expert", "dp"), None),
            P(("expert", "dp"), None),
            P("expert", "dp", None),
            P("expert", None, "dp"),
        ),
        check_vma=False,
    )
```

```python
import functools

import jax
import jax.numpy as jnp
from jax import lax
from jax.experimental import pallas as pl
from jax.experimental.pallas import tpu as pltpu
from jax.sharding import PartitionSpec as P

MESH = pl.DeviceIdType.MESH
SIDE = 2
PLANE = SIDE * SIDE

beta_one = 0.9
beta_two = 0.95
epsilon = 1e-08


def expert_forward(rows_x, w_gu):
    hidden = w_gu.shape[1] // 2
    both = jnp.dot(rows_x, w_gu, preferred_element_type=jnp.float32)
    gate = both[:, :hidden]
    upper = both[:, hidden:]
    activated = (gate * jax.nn.sigmoid(gate) * upper).astype(jnp.bfloat16)
    return (both, activated)


def expert_output(activated, w_down):
    return jnp.dot(activated, w_down, preferred_element_type=jnp.float32).astype(jnp.bfloat16)


def expert_backward(rows_x, rows_cot, both, activated, w_down):
    hidden = w_down.shape[0]
    gate = both[:, :hidden]
    upper = both[:, hidden:]
    sigmoid_gate = jax.nn.sigmoid(gate)
    grad_act = lax.dot_general(
        rows_cot, w_down, (((1,), (1,)), ((), ())), preferred_element_type=jnp.float32
    )
    grad_gate = grad_act * upper * (sigmoid_gate * (1.0 + gate * (1.0 - sigmoid_gate)))
    grad_upper = grad_act * gate * sigmoid_gate
    grad_both = jnp.concatenate([grad_gate, grad_upper], axis=1).astype(jnp.bfloat16)
    grad_gu = lax.dot_general(
        rows_x, grad_both, (((0,), (0,)), ((), ())), preferred_element_type=jnp.float32
    )
    grad_down = lax.dot_general(
        activated, rows_cot, (((0,), (0,)), ((), ())), preferred_element_type=jnp.float32
    )
    return (grad_both, grad_gu, grad_down)


def expert_row_grad(grad_both, w_gu):
    return lax.dot_general(
        grad_both, w_gu, (((1,), (1,)), ((), ())), preferred_element_type=jnp.float32
    ).astype(jnp.bfloat16)


def adam_direction(first, second, grad):
    first_new = beta_one * first.astype(jnp.float32) + (1.0 - beta_one) * grad
    second_new = beta_two * second.astype(jnp.float32) + (1.0 - beta_two) * grad * grad
    first_fix = 1.0 - beta_one**10.0
    second_fix = 1.0 - beta_two**10.0
    return (first_new / first_fix / (jnp.sqrt(second_new / second_fix) + epsilon)).astype(
        jnp.bfloat16
    )


def pack(step_gu, step_down):
    wide = step_gu.shape[1]
    rest = step_down.shape[1] - wide
    tail = step_down[:, wide:].reshape(wide // rest, -1, rest)
    beside = jnp.concatenate([tail[i] for i in range(wide // rest)], axis=1)
    return jnp.concatenate([step_gu, step_down[:, :wide], beside], axis=0)


def unpack(rows, step_gu, step_down):
    wide = step_gu.shape[1]
    rest = step_down.shape[1] - wide
    upper = step_gu.shape[0]
    lower = upper + step_down.shape[0]
    tail = jnp.concatenate(
        [rows[lower:, i * rest : (i + 1) * rest] for i in range(wide // rest)], axis=0
    )
    return (rows[:upper], jnp.concatenate([rows[upper:lower], tail], axis=1))


def exchange(pieces):
    return lax.all_to_all(pieces, "expert", split_axis=0, concat_axis=0, tiled=True)


def position(count):
    deep = count // PLANE
    me = lax.axis_index("expert")
    return (deep, me // PLANE, (me // SIDE) % SIDE, me % SIDE)


def slot_of(z, y, x):
    return z * PLANE + y * SIDE + x


def greet(partners):
    barrier = pltpu.get_barrier_semaphore()
    for partner in partners:
        pl.semaphore_signal(barrier, inc=1, device_id=partner, device_id_type=MESH)
    pl.semaphore_wait(barrier, len(partners))


def gather_kernel(count, *refs):
    tensors = 2
    sources, outs = refs[:tensors], refs[tensors : 2 * tensors]
    own_sem, z_send, z_recv, xy_send, xy_recv, d_send, d_recv = refs[2 * tensors :]
    deep, z, y, x = position(count)
    core = lax.axis_index("dp")
    half = sources[0].shape[0] // 2
    up = [(slot_of((z + k) % deep, y, x), core) for k in range(deep)]
    beside = ((slot_of(z, y, 1 - x), core), (slot_of(z, 1 - y, x), core))
    greet(up[1:] + list(beside))

    def copy(src, dst, send, recv, device):
        return pltpu.make_async_remote_copy(
            src_ref=src, dst_ref=dst, send_sem=send, recv_sem=recv,
            device_id=device, device_id_type=MESH,
        )

    def across(t, k, origin):
        return copy(sources[t], outs[t].at[origin], z_send.at[t, k - 1], z_recv.at[t, k - 1], up[k])

    def to_side(t, k, way, src, origin):
        return copy(
            src, outs[t].at[origin], xy_send.at[t, k, way], xy_recv.at[t, k, way], beside[way]
        )

    def onward(t, k, way, origin):
        rows = pl.ds(way * half, half)
        piece = outs[t].at[origin, rows]
        return copy(piece, piece, d_send.at[t, k, way], d_recv.at[t, k, way], beside[1 - way])

    me = slot_of(z, y, x)
    sent = []
    locals_ = []
    for t in range(tensors):
        own = pltpu.make_async_copy(sources[t], outs[t].at[me], own_sem.at[t])
        own.start()
        locals_.append(own)
    for t in range(tensors):
        for way in range(2):
            step = to_side(t, 0, way, sources[t], me)
            step.start()
            sent.append(step)
        for k in range(1, deep):
            step = across(t, k, me)
            step.start()
            sent.append(step)

    def forward(t, k):
        zk = (z - k + deep) % deep
        came = (slot_of(zk, y, 1 - x), slot_of(zk, 1 - y, x))
        for way in range(2):
            to_side(t, k, way, outs[t].at[came[way]], came[way]).wait_recv()
            step = onward(t, k, way, came[way])
            step.start()
            sent.append(step)

    for t in range(tensors):
        for k in range(1, deep):
            origin = slot_of((z - k + deep) % deep, y, x)
            across(t, k, origin).wait_recv()
            for way in range(2):
                step = to_side(t, k, way, outs[t].at[origin], origin)
                step.start()
                sent.append(step)
            forward(t, k - 1)
        forward(t, deep - 1)
    for t in range(tensors):
        for k in range(deep):
            zk = (z - k + deep) % deep
            for way in range(2):
                onward(t, k, way, slot_of(zk, 1 - y, 1 - x)).wait_recv()
    for own in locals_:
        own.wait()
    for step in sent:
        step.wait_send()


def gather_rows(tokens, out_grad):
    count = lax.axis_size("expert")
    rows, width = tokens.shape
    deep = count // PLANE
    dma = pltpu.SemaphoreType.DMA
    full = jax.ShapeDtypeStruct((count, rows, width), tokens.dtype)
    got = pl.pallas_call(
        functools.partial(gather_kernel, count),
        out_shape=(full, full),
        in_specs=[pl.BlockSpec(memory_space=pl.ANY)] * 2,
        out_specs=(pl.BlockSpec(memory_space=pl.ANY),) * 2,
        scratch_shapes=[
            dma((2,)),
            dma((2, deep - 1)),
            dma((2, deep - 1)),
            dma((2, deep, 2)),
            dma((2, deep, 2)),
            dma((2, deep, 2)),
            dma((2, deep, 2)),
        ],
        compiler_params=pltpu.CompilerParams(collective_id=0, has_side_effects=True),
    )(tokens, out_grad)
    return tuple(part.reshape(count * rows, width) for part in got)


def sum_kernel(count, *refs):
    tensors = 2
    parts, leaving = refs[:tensors], refs[tensors]
    outs, landed = refs[tensors + 1 : 2 * tensors + 1], refs[2 * tensors + 1]
    (got_d, got_xy, got_z, out_xy, out_z,
     z_send, z_recv, xy_send, xy_recv, d_send, d_recv,
     leg_send, leg_recv, own_sem) = refs[2 * tensors + 2 :]
    deep, z, y, x = position(count)
    core = lax.axis_index("dp")
    half = outs[0].shape[0] // 2
    up = [(slot_of((z + k) % deep, y, x), core) for k in range(deep)]
    beside = ((slot_of(z, y, 1 - x), core), (slot_of(z, 1 - y, x), core))
    me = slot_of(z, y, x)
    others = [lax.rem(me + j, count) for j in range(1, count)]
    greet([(other, core) for other in others])

    def copy(src, dst, send, recv, device):
        return pltpu.make_async_remote_copy(
            src_ref=src, dst_ref=dst, send_sem=send, recv_sem=recv,
            device_id=device, device_id_type=MESH,
        )

    def wide(ref, index):
        return ref[index].astype(jnp.float32)

    order = [(k + 1) % deep for k in range(deep)]
    jobs = [(t, k) for t in range(tensors) for k in order]
    sent = []
    first = {}
    for t, k in jobs:
        far = slot_of((z + k) % deep, 1 - y, 1 - x)
        for way in range(2):
            step = copy(
                parts[t].at[far, pl.ds(way * half, half)], got_d.at[t, k, way],
                d_send.at[t, k, way], d_recv.at[t, k, way], beside[1 - way],
            )
            step.start()
            first[t, k, way] = step
            sent.append(step)
    own = pltpu.make_async_copy(leaving.at[me], landed.at[me], own_sem)
    own.start()
    legs = []
    for j, other in enumerate(others):
        step = copy(
            leaving.at[other], landed.at[me], leg_send.at[j], leg_recv.at[j], (other, core)
        )
        step.start()
        legs.append(step)
    second = {}

    def pass_on(t, k):
        zk = (z + k) % deep
        near = (slot_of(zk, y, 1 - x), slot_of(zk, 1 - y, x))
        for way in range(2):
            first[t, k, way].wait_recv()
            rows, rest = pl.ds(way * half, half), pl.ds((1 - way) * half, half)
            total = wide(parts[t], (near[way], rows)) + wide(got_d, (t, k, way))
            out_xy[t, k, way, rows] = total.astype(jnp.bfloat16)
            out_xy[t, k, way, rest] = parts[t][near[way], rest]
            step = copy(
                out_xy.at[t, k, way], got_xy.at[t, k, way],
                xy_send.at[t, k, way], xy_recv.at[t, k, way], beside[way],
            )
            step.start()
            second[t, k, way] = step
            sent.append(step)

    third = {}

    def plane_sum(t, k):
        second[t, k, 0].wait_recv()
        second[t, k, 1].wait_recv()
        total = wide(got_xy, (t, k, 0)) + wide(got_xy, (t, k, 1))
        return total + wide(parts[t], slot_of((z + k) % deep, y, x))

    def leave(t, k):
        if k == 0:
            return
        out_z[t, k - 1] = plane_sum(t, k).astype(jnp.bfloat16)
        step = copy(
            out_z.at[t, k - 1], got_z.at[t, k - 1], z_send.at[t, k - 1], z_recv.at[t, k - 1], up[k]
        )
        step.start()
        third[t, k] = step
        sent.append(step)

    pass_on(*jobs[0])
    for now, after in zip(jobs, jobs[1:]):
        pass_on(*after)
        leave(*now)
    for t in range(tensors):
        total = plane_sum(t, 0)
        for k in range(1, deep):
            third[t, k].wait_recv()
            total = total + wide(got_z, (t, k - 1))
        outs[t][...] = total.astype(jnp.bfloat16)
    for j, step in enumerate(legs):
        origin = lax.rem(me + count - j - 1, count)
        copy(
            leaving.at[origin], landed.at[origin], leg_send.at[j], leg_recv.at[j],
            (others[j], core),
        ).wait_recv()
    own.wait()
    for step in sent + legs:
        step.wait_send()


def sum_rows(part_out, part_grad, leaving):
    count = lax.axis_size("expert")
    rows, width = part_out.shape[0] // count, part_out.shape[1]
    deep = count // PLANE
    dma = pltpu.SemaphoreType.DMA
    block = jax.ShapeDtypeStruct((rows, width), part_out.dtype)
    vmem = lambda *lead: pltpu.VMEM(lead + (width,), jnp.bfloat16)
    return pl.pallas_call(
        functools.partial(sum_kernel, count),
        out_shape=(block, block, jax.ShapeDtypeStruct(leaving.shape, leaving.dtype)),
        in_specs=[pl.BlockSpec(memory_space=pltpu.VMEM)] * 2 + [pl.BlockSpec(memory_space=pl.ANY)],
        out_specs=(pl.BlockSpec(memory_space=pltpu.VMEM),) * 2
        + (pl.BlockSpec(memory_space=pl.ANY),),
        scratch_shapes=[
            vmem(2, deep, 2, rows // 2),
            vmem(2, deep, 2, rows),
            vmem(2, deep - 1, rows),
            vmem(2, deep, 2, rows),
            vmem(2, deep - 1, rows),
            dma((2, deep - 1)),
            dma((2, deep - 1)),
            dma((2, deep, 2)),
            dma((2, deep, 2)),
            dma((2, deep, 2)),
            dma((2, deep, 2)),
            dma((count - 1,)),
            dma((count - 1,)),
            dma,
        ],
        compiler_params=pltpu.CompilerParams(
            collective_id=1, has_side_effects=True, vmem_limit_bytes=56 * 1024 * 1024
        ),
    )(part_out.reshape(count, rows, width), part_grad.reshape(count, rows, width), leaving)


def rows_by_gather(tokens, out_grad, target, probs, w_gu, w_down, relocate):
    count = lax.axis_size("expert")
    lanes = jnp.arange(count, dtype=jnp.int32)
    chosen = target[:, :, None] == lanes[None, None, :]
    weights = jnp.sum(jnp.where(chosen, probs[:, :, None], 0.0), axis=1).T
    prob_in = lax.all_to_all(weights, "expert", split_axis=0, concat_axis=0, tiled=True)
    rows_x, rows_g = gather_rows(tokens, out_grad)
    prob = prob_in.reshape(-1, 1)
    both, activated = expert_forward(rows_x, w_gu)
    rows_cot = (prob * rows_g.astype(jnp.float32)).astype(jnp.bfloat16)
    grad_both, grad_gu, grad_down = expert_backward(rows_x, rows_cot, both, activated, w_down)
    step, pieces, ordered = relocate(grad_gu, grad_down)
    activated, grad_both, _ = lax.optimization_barrier((activated, grad_both, step))
    output = expert_output(activated, w_down)
    part_out = (prob * output.astype(jnp.float32)).astype(jnp.bfloat16)
    row_grad = expert_row_grad(grad_both, w_gu)
    mixed, token_grad, landed = sum_rows(part_out, row_grad, ordered)
    return (mixed, token_grad, landed)


def rows_by_exchange(tokens, out_grad, target, probs, w_gu, w_down, relocate):
    count = lax.axis_size("expert")
    tok_rows, width = tokens.shape
    top = target.shape[1]
    capacity = max(2, tok_rows * top * 9 // (8 * count))
    rows = count * capacity
    lanes = jnp.arange(count, dtype=jnp.int32)
    flat_target = target.reshape(-1)
    onehot = (flat_target[:, None] == lanes[None, :]).astype(jnp.int32)
    place = jnp.sum(onehot * (jnp.cumsum(onehot, axis=0) - 1), axis=1)
    slot = flat_target * capacity + place
    match = slot[None, :] == jnp.arange(rows, dtype=jnp.int32)[:, None]
    pick = jnp.any(match.reshape(rows, tok_rows, top), axis=2).astype(jnp.bfloat16)
    slot_prob = jnp.sum(jnp.where(match, probs.reshape(1, -1), 0.0), axis=1)
    send_x = (
        jnp.dot(pick, tokens, preferred_element_type=jnp.float32)
        .astype(jnp.bfloat16)
        .reshape(count, capacity, width)
    )
    send_cot = (
        (jnp.dot(pick, out_grad, preferred_element_type=jnp.float32) * slot_prob[:, None])
        .astype(jnp.bfloat16)
        .reshape(count, capacity, width)
    )
    recv_x = lax.all_to_all(send_x, "expert", split_axis=0, concat_axis=0, tiled=True)
    rows_x = recv_x.reshape(rows, width)
    both, activated = expert_forward(rows_x, w_gu)
    output = expert_output(activated, w_down)
    back_out = lax.all_to_all(
        output.reshape(count, capacity, width), "expert", split_axis=0, concat_axis=0, tiled=True
    )
    recv_cot = lax.all_to_all(send_cot, "expert", split_axis=0, concat_axis=0, tiled=True)
    rows_cot = recv_cot.reshape(rows, width)
    grad_both, grad_gu, grad_down = expert_backward(rows_x, rows_cot, both, activated, w_down)
    row_grad = expert_row_grad(grad_both, w_gu)
    back_grad = lax.all_to_all(
        row_grad.reshape(count, capacity, width), "expert", split_axis=0, concat_axis=0, tiled=True
    )
    back_pick = lambda weight, piece: lax.dot_general(
        weight.astype(jnp.bfloat16),
        piece.reshape(rows, width),
        (((0,), (0,)), ((), ())),
        preferred_element_type=jnp.float32,
    )
    weight = pick.astype(jnp.float32) * slot_prob[:, None]
    coarse = lax.reduce_precision(weight, 8, 7)
    mixed = (back_pick(coarse, back_out) + back_pick(weight - coarse, back_out)).astype(jnp.bfloat16)
    token_grad = back_pick(pick, back_grad).astype(jnp.bfloat16)
    return (mixed, token_grad, exchange(relocate(grad_gu, grad_down)[2]))


def per_device(
    tokens,
    out_grad,
    expert_ids,
    route_scores,
    old_slot,
    new_slot,
    gate_up,
    down,
    first_gu,
    second_gu,
    first_down,
    second_down,
):
    count = lax.axis_size("expert")
    lanes = jnp.arange(count, dtype=jnp.int32)
    owner = new_slot[None, :] == lanes[:, None]
    source = jnp.sum(jnp.where(owner, old_slot[None, :], 0), axis=1)
    probs = route_scores / jnp.sum(route_scores, axis=1, keepdims=True)
    target = jnp.sum(
        jnp.where(expert_ids[:, :, None] == lanes[None, None, :], old_slot[None, None, :], 0),
        axis=2,
    )
    gathered = count % (2 * PLANE) == 0 and 2 * expert_ids.shape[1] >= count
    rows_plan = rows_by_gather if gathered else rows_by_exchange

    def relocate(grad_gu, grad_down):
        share_gu, share_down = (
            lax.psum_scatter(
                grad_gu.astype(jnp.bfloat16), "dp", scatter_dimension=0, tiled=True
            ).astype(jnp.float32),
            lax.psum_scatter(
                grad_down.astype(jnp.bfloat16), "dp", scatter_dimension=1, tiled=True
            ).astype(jnp.float32),
        )
        step_gu = adam_direction(first_gu[0], second_gu[0], share_gu)
        step_down = adam_direction(first_down[0], second_down[0], share_down)
        step = pack(step_gu, step_down)
        pieces = exchange(step.reshape(count, -1, step.shape[1]))
        return (step, pieces, jnp.take(pieces, source, axis=0, mode="clip"))

    mixed, token_grad, landed = rows_plan(
        tokens, out_grad, target, probs, gate_up[0], down[0], relocate
    )
    update_gu, update_down = unpack(
        landed.reshape(-1, landed.shape[2]), first_gu[0], first_down[0]
    )
    return (mixed, token_grad, update_gu[None], update_down[None])


def solution(mesh):
    placed = (
        P(("expert", "dp"), None),
        P(("expert", "dp"), None),
        P(("expert", "dp"), None),
        P(("expert", "dp"), None),
        P(),
        P(),
        P("expert", None, None),
        P("expert", None, None),
        P("expert", "dp", None),
        P("expert", "dp", None),
        P("expert", None, "dp"),
        P("expert", None, "dp"),
    )
    return jax.shard_map(
        per_device,
        mesh=mesh,
        in_specs=placed,
        out_specs=(
            P(("expert", "dp"), None),
            P(("expert", "dp"), None),
            P("expert", "dp", None),
            P("expert", None, "dp"),
        ),
        check_vma=False,
    )
```

```python
import functools

import jax
import jax.numpy as jnp
from jax import lax
from jax.experimental import pallas as pl
from jax.experimental.pallas import tpu as pltpu
from jax.sharding import PartitionSpec as P

MESH = pl.DeviceIdType.MESH
SIDE = 2
PLANE = SIDE * SIDE

beta_one = 0.9
beta_two = 0.95
epsilon = 1e-08


def expert_forward(rows_x, w_gu):
    hidden = w_gu.shape[1] // 2
    both = jnp.dot(rows_x, w_gu, preferred_element_type=jnp.float32)
    gate = both[:, :hidden]
    upper = both[:, hidden:]
    activated = (gate * jax.nn.sigmoid(gate) * upper).astype(jnp.bfloat16)
    return (both, activated)


def expert_output(activated, w_down):
    return jnp.dot(activated, w_down, preferred_element_type=jnp.float32).astype(jnp.bfloat16)


def expert_backward(rows_x, rows_cot, both, activated, w_down):
    hidden = w_down.shape[0]
    gate = both[:, :hidden]
    upper = both[:, hidden:]
    sigmoid_gate = jax.nn.sigmoid(gate)
    grad_act = lax.dot_general(
        rows_cot, w_down, (((1,), (1,)), ((), ())), preferred_element_type=jnp.float32
    )
    grad_gate = grad_act * upper * (sigmoid_gate * (1.0 + gate * (1.0 - sigmoid_gate)))
    grad_upper = grad_act * gate * sigmoid_gate
    grad_both = jnp.concatenate([grad_gate, grad_upper], axis=1).astype(jnp.bfloat16)
    grad_gu = lax.dot_general(
        rows_x, grad_both, (((0,), (0,)), ((), ())), preferred_element_type=jnp.float32
    )
    grad_down = lax.dot_general(
        activated, rows_cot, (((0,), (0,)), ((), ())), preferred_element_type=jnp.float32
    )
    return (grad_both, grad_gu, grad_down)


def expert_row_grad(grad_both, w_gu):
    return lax.dot_general(
        grad_both, w_gu, (((1,), (1,)), ((), ())), preferred_element_type=jnp.float32
    ).astype(jnp.bfloat16)


def adam_direction(first, second, grad):
    first_new = beta_one * first.astype(jnp.float32) + (1.0 - beta_one) * grad
    second_new = beta_two * second.astype(jnp.float32) + (1.0 - beta_two) * grad * grad
    first_fix = 1.0 - beta_one**10.0
    second_fix = 1.0 - beta_two**10.0
    return (first_new / first_fix / (jnp.sqrt(second_new / second_fix) + epsilon)).astype(
        jnp.bfloat16
    )


def pack(step_gu, step_down):
    wide = step_gu.shape[1]
    rest = step_down.shape[1] - wide
    tail = step_down[:, wide:].reshape(wide // rest, -1, rest)
    beside = jnp.concatenate([tail[i] for i in range(wide // rest)], axis=1)
    return jnp.concatenate([step_gu, step_down[:, :wide], beside], axis=0)


def unpack(rows, step_gu, step_down):
    wide = step_gu.shape[1]
    rest = step_down.shape[1] - wide
    upper = step_gu.shape[0]
    lower = upper + step_down.shape[0]
    tail = jnp.concatenate(
        [rows[lower:, i * rest : (i + 1) * rest] for i in range(wide // rest)], axis=0
    )
    return (rows[:upper], jnp.concatenate([rows[upper:lower], tail], axis=1))


def exchange(pieces):
    return lax.all_to_all(pieces, "expert", split_axis=0, concat_axis=0, tiled=True)


def position(count):
    deep = count // PLANE
    me = lax.axis_index("expert")
    return (deep, me // PLANE, (me // SIDE) % SIDE, me % SIDE)


def slot_of(z, y, x):
    return z * PLANE + y * SIDE + x


def greet(partners):
    barrier = pltpu.get_barrier_semaphore()
    for partner in partners:
        pl.semaphore_signal(barrier, inc=1, device_id=partner, device_id_type=MESH)
    pl.semaphore_wait(barrier, len(partners))


def gather_kernel(count, *refs):
    tensors = 2
    sources, outs = refs[:tensors], refs[tensors : 2 * tensors]
    own_sem, z_send, z_recv, xy_send, xy_recv, d_send, d_recv = refs[2 * tensors :]
    deep, z, y, x = position(count)
    core = lax.axis_index("dp")
    half = sources[0].shape[0] // 2
    up = [(slot_of((z + k) % deep, y, x), core) for k in range(deep)]
    beside = ((slot_of(z, y, 1 - x), core), (slot_of(z, 1 - y, x), core))
    greet(up[1:] + list(beside))

    def copy(src, dst, send, recv, device):
        return pltpu.make_async_remote_copy(
            src_ref=src, dst_ref=dst, send_sem=send, recv_sem=recv,
            device_id=device, device_id_type=MESH,
        )

    def across(t, k, origin):
        return copy(sources[t], outs[t].at[origin], z_send.at[t, k - 1], z_recv.at[t, k - 1], up[k])

    def to_side(t, k, way, src, origin):
        return copy(
            src, outs[t].at[origin], xy_send.at[t, k, way], xy_recv.at[t, k, way], beside[way]
        )

    def onward(t, k, way, origin):
        rows = pl.ds(way * half, half)
        piece = outs[t].at[origin, rows]
        return copy(piece, piece, d_send.at[t, k, way], d_recv.at[t, k, way], beside[1 - way])

    me = slot_of(z, y, x)
    sent = []
    locals_ = []
    for t in range(tensors):
        own = pltpu.make_async_copy(sources[t], outs[t].at[me], own_sem.at[t])
        own.start()
        locals_.append(own)
    for t in range(tensors):
        for way in range(2):
            step = to_side(t, 0, way, sources[t], me)
            step.start()
            sent.append(step)
        for k in range(1, deep):
            step = across(t, k, me)
            step.start()
            sent.append(step)

    def forward(t, k):
        zk = (z - k + deep) % deep
        came = (slot_of(zk, y, 1 - x), slot_of(zk, 1 - y, x))
        for way in range(2):
            to_side(t, k, way, outs[t].at[came[way]], came[way]).wait_recv()
            step = onward(t, k, way, came[way])
            step.start()
            sent.append(step)

    for t in range(tensors):
        for k in range(1, deep):
            origin = slot_of((z - k + deep) % deep, y, x)
            across(t, k, origin).wait_recv()
            for way in range(2):
                step = to_side(t, k, way, outs[t].at[origin], origin)
                step.start()
                sent.append(step)
            forward(t, k - 1)
        forward(t, deep - 1)
    for t in range(tensors):
        for k in range(deep):
            zk = (z - k + deep) % deep
            for way in range(2):
                onward(t, k, way, slot_of(zk, 1 - y, 1 - x)).wait_recv()
    for own in locals_:
        own.wait()
    for step in sent:
        step.wait_send()


def gather_rows(tokens, out_grad):
    count = lax.axis_size("expert")
    rows, width = tokens.shape
    deep = count // PLANE
    dma = pltpu.SemaphoreType.DMA
    full = jax.ShapeDtypeStruct((count, rows, width), tokens.dtype)
    got = pl.pallas_call(
        functools.partial(gather_kernel, count),
        out_shape=(full, full),
        in_specs=[pl.BlockSpec(memory_space=pl.ANY)] * 2,
        out_specs=(pl.BlockSpec(memory_space=pl.ANY),) * 2,
        scratch_shapes=[
            dma((2,)),
            dma((2, deep - 1)),
            dma((2, deep - 1)),
            dma((2, deep, 2)),
            dma((2, deep, 2)),
            dma((2, deep, 2)),
            dma((2, deep, 2)),
        ],
        compiler_params=pltpu.CompilerParams(collective_id=0, has_side_effects=True),
    )(tokens, out_grad)
    return tuple(part.reshape(count * rows, width) for part in got)


def sum_kernel(count, *refs):
    tensors = 2
    parts, leaving = refs[:tensors], refs[tensors]
    outs, landed = refs[tensors + 1 : 2 * tensors + 1], refs[2 * tensors + 1]
    (got_d, got_xy, got_z, out_xy, out_z,
     z_send, z_recv, xy_send, xy_recv, d_send, d_recv,
     leg_send, leg_recv, own_sem) = refs[2 * tensors + 2 :]
    deep, z, y, x = position(count)
    core = lax.axis_index("dp")
    half = outs[0].shape[0] // 2
    up = [(slot_of((z + k) % deep, y, x), core) for k in range(deep)]
    beside = ((slot_of(z, y, 1 - x), core), (slot_of(z, 1 - y, x), core))
    me = slot_of(z, y, x)
    others = [lax.rem(me + j, count) for j in range(1, count)]
    greet([(other, core) for other in others])

    def copy(src, dst, send, recv, device):
        return pltpu.make_async_remote_copy(
            src_ref=src, dst_ref=dst, send_sem=send, recv_sem=recv,
            device_id=device, device_id_type=MESH,
        )

    def wide(ref, index):
        return ref[index].astype(jnp.float32)

    order = [(k + 1) % deep for k in range(deep)]
    jobs = [(t, k) for t in range(tensors) for k in order]
    sent = []
    first = {}
    for t, k in jobs:
        far = slot_of((z + k) % deep, 1 - y, 1 - x)
        for way in range(2):
            step = copy(
                parts[t].at[far, pl.ds(way * half, half)], got_d.at[t, k, way],
                d_send.at[t, k, way], d_recv.at[t, k, way], beside[1 - way],
            )
            step.start()
            first[t, k, way] = step
            sent.append(step)
    own = pltpu.make_async_copy(leaving.at[me], landed.at[me], own_sem)
    own.start()
    legs = []
    for j, other in enumerate(others):
        step = copy(
            leaving.at[other], landed.at[me], leg_send.at[j], leg_recv.at[j], (other, core)
        )
        step.start()
        legs.append(step)
    second = {}

    def pass_on(t, k):
        zk = (z + k) % deep
        near = (slot_of(zk, y, 1 - x), slot_of(zk, 1 - y, x))
        for way in range(2):
            first[t, k, way].wait_recv()
            rows, rest = pl.ds(way * half, half), pl.ds((1 - way) * half, half)
            total = wide(parts[t], (near[way], rows)) + wide(got_d, (t, k, way))
            out_xy[t, k, way, rows] = total.astype(jnp.bfloat16)
            out_xy[t, k, way, rest] = parts[t][near[way], rest]
            step = copy(
                out_xy.at[t, k, way], got_xy.at[t, k, way],
                xy_send.at[t, k, way], xy_recv.at[t, k, way], beside[way],
            )
            step.start()
            second[t, k, way] = step
            sent.append(step)

    third = {}

    def plane_sum(t, k):
        second[t, k, 0].wait_recv()
        second[t, k, 1].wait_recv()
        total = wide(got_xy, (t, k, 0)) + wide(got_xy, (t, k, 1))
        return total + wide(parts[t], slot_of((z + k) % deep, y, x))

    def leave(t, k):
        if k == 0:
            return
        out_z[t, k - 1] = plane_sum(t, k).astype(jnp.bfloat16)
        step = copy(
            out_z.at[t, k - 1], got_z.at[t, k - 1], z_send.at[t, k - 1], z_recv.at[t, k - 1], up[k]
        )
        step.start()
        third[t, k] = step
        sent.append(step)

    pass_on(*jobs[0])
    for now, after in zip(jobs, jobs[1:]):
        pass_on(*after)
        leave(*now)
    for t in range(tensors):
        total = plane_sum(t, 0)
        for k in range(1, deep):
            third[t, k].wait_recv()
            total = total + wide(got_z, (t, k - 1))
        outs[t][...] = total.astype(jnp.bfloat16)
    for j, step in enumerate(legs):
        origin = lax.rem(me + count - j - 1, count)
        copy(
            leaving.at[origin], landed.at[origin], leg_send.at[j], leg_recv.at[j],
            (others[j], core),
        ).wait_recv()
    own.wait()
    for step in sent + legs:
        step.wait_send()


def sum_rows(part_out, part_grad, leaving):
    count = lax.axis_size("expert")
    rows, width = part_out.shape[0] // count, part_out.shape[1]
    deep = count // PLANE
    dma = pltpu.SemaphoreType.DMA
    block = jax.ShapeDtypeStruct((rows, width), part_out.dtype)
    vmem = lambda *lead: pltpu.VMEM(lead + (width,), jnp.bfloat16)
    return pl.pallas_call(
        functools.partial(sum_kernel, count),
        out_shape=(block, block, jax.ShapeDtypeStruct(leaving.shape, leaving.dtype)),
        in_specs=[pl.BlockSpec(memory_space=pltpu.VMEM)] * 2 + [pl.BlockSpec(memory_space=pl.ANY)],
        out_specs=(pl.BlockSpec(memory_space=pltpu.VMEM),) * 2
        + (pl.BlockSpec(memory_space=pl.ANY),),
        scratch_shapes=[
            vmem(2, deep, 2, rows // 2),
            vmem(2, deep, 2, rows),
            vmem(2, deep - 1, rows),
            vmem(2, deep, 2, rows),
            vmem(2, deep - 1, rows),
            dma((2, deep - 1)),
            dma((2, deep - 1)),
            dma((2, deep, 2)),
            dma((2, deep, 2)),
            dma((2, deep, 2)),
            dma((2, deep, 2)),
            dma((count - 1,)),
            dma((count - 1,)),
            dma,
        ],
        compiler_params=pltpu.CompilerParams(
            collective_id=1, has_side_effects=True, vmem_limit_bytes=56 * 1024 * 1024
        ),
    )(part_out.reshape(count, rows, width), part_grad.reshape(count, rows, width), leaving)


def rows_by_gather(tokens, out_grad, target, probs, w_gu, w_down, relocate):
    count = lax.axis_size("expert")
    lanes = jnp.arange(count, dtype=jnp.int32)
    chosen = target[:, :, None] == lanes[None, None, :]
    weights = jnp.sum(jnp.where(chosen, probs[:, :, None], 0.0), axis=1).T
    prob_in = lax.all_to_all(weights, "expert", split_axis=0, concat_axis=0, tiled=True)
    rows_x, rows_g = gather_rows(tokens, out_grad)
    prob = prob_in.reshape(-1, 1)
    both, activated = expert_forward(rows_x, w_gu)
    rows_cot = lax.optimization_barrier((prob * rows_g.astype(jnp.float32)).astype(jnp.bfloat16))
    grad_both, grad_gu, grad_down = expert_backward(rows_x, rows_cot, both, activated, w_down)
    step, pieces, ordered = relocate(grad_gu, grad_down)
    activated, grad_both, _ = lax.optimization_barrier((activated, grad_both, step))
    output = expert_output(activated, w_down)
    part_out = (prob * output.astype(jnp.float32)).astype(jnp.bfloat16)
    row_grad = expert_row_grad(grad_both, w_gu)
    mixed, token_grad, landed = sum_rows(part_out, row_grad, ordered)
    return (mixed, token_grad, landed)


def rows_by_exchange(tokens, out_grad, target, probs, w_gu, w_down, relocate):
    count = lax.axis_size("expert")
    tok_rows, width = tokens.shape
    top = target.shape[1]
    capacity = max(2, tok_rows * top * 9 // (8 * count))
    rows = count * capacity
    lanes = jnp.arange(count, dtype=jnp.int32)
    flat_target = target.reshape(-1)
    onehot = (flat_target[:, None] == lanes[None, :]).astype(jnp.int32)
    place = jnp.sum(onehot * (jnp.cumsum(onehot, axis=0) - 1), axis=1)
    slot = flat_target * capacity + place
    match = slot[None, :] == jnp.arange(rows, dtype=jnp.int32)[:, None]
    pick = jnp.any(match.reshape(rows, tok_rows, top), axis=2).astype(jnp.bfloat16)
    slot_prob = jnp.sum(jnp.where(match, probs.reshape(1, -1), 0.0), axis=1)
    send_x = (
        jnp.dot(pick, tokens, preferred_element_type=jnp.float32)
        .astype(jnp.bfloat16)
        .reshape(count, capacity, width)
    )
    send_cot = (
        (jnp.dot(pick, out_grad, preferred_element_type=jnp.float32) * slot_prob[:, None])
        .astype(jnp.bfloat16)
        .reshape(count, capacity, width)
    )
    recv_x = lax.all_to_all(send_x, "expert", split_axis=0, concat_axis=0, tiled=True)
    rows_x = recv_x.reshape(rows, width)
    both, activated = expert_forward(rows_x, w_gu)
    output = expert_output(activated, w_down)
    back_out = lax.all_to_all(
        output.reshape(count, capacity, width), "expert", split_axis=0, concat_axis=0, tiled=True
    )
    recv_cot = lax.all_to_all(send_cot, "expert", split_axis=0, concat_axis=0, tiled=True)
    rows_cot = recv_cot.reshape(rows, width)
    grad_both, grad_gu, grad_down = expert_backward(rows_x, rows_cot, both, activated, w_down)
    row_grad = expert_row_grad(grad_both, w_gu)
    back_grad = lax.all_to_all(
        row_grad.reshape(count, capacity, width), "expert", split_axis=0, concat_axis=0, tiled=True
    )
    back_pick = lambda weight, piece: lax.dot_general(
        weight.astype(jnp.bfloat16),
        piece.reshape(rows, width),
        (((0,), (0,)), ((), ())),
        preferred_element_type=jnp.float32,
    )
    weight = pick.astype(jnp.float32) * slot_prob[:, None]
    coarse = lax.reduce_precision(weight, 8, 7)
    mixed = (back_pick(coarse, back_out) + back_pick(weight - coarse, back_out)).astype(jnp.bfloat16)
    token_grad = back_pick(pick, back_grad).astype(jnp.bfloat16)
    return (mixed, token_grad, exchange(relocate(grad_gu, grad_down)[2]))


def per_device(
    tokens,
    out_grad,
    expert_ids,
    route_scores,
    old_slot,
    new_slot,
    gate_up,
    down,
    first_gu,
    second_gu,
    first_down,
    second_down,
):
    count = lax.axis_size("expert")
    lanes = jnp.arange(count, dtype=jnp.int32)
    owner = new_slot[None, :] == lanes[:, None]
    source = jnp.sum(jnp.where(owner, old_slot[None, :], 0), axis=1)
    probs = route_scores / jnp.sum(route_scores, axis=1, keepdims=True)
    target = jnp.sum(
        jnp.where(expert_ids[:, :, None] == lanes[None, None, :], old_slot[None, None, :], 0),
        axis=2,
    )
    gathered = count % (2 * PLANE) == 0 and 2 * expert_ids.shape[1] >= count
    rows_plan = rows_by_gather if gathered else rows_by_exchange

    def relocate(grad_gu, grad_down):
        share_gu, share_down = (
            lax.psum_scatter(
                grad_gu.astype(jnp.bfloat16), "dp", scatter_dimension=0, tiled=True
            ).astype(jnp.float32),
            lax.psum_scatter(
                grad_down.astype(jnp.bfloat16), "dp", scatter_dimension=1, tiled=True
            ).astype(jnp.float32),
        )
        step_gu = adam_direction(first_gu[0], second_gu[0], share_gu)
        step_down = adam_direction(first_down[0], second_down[0], share_down)
        step = pack(step_gu, step_down)
        pieces = exchange(step.reshape(count, -1, step.shape[1]))
        return (step, pieces, jnp.take(pieces, source, axis=0, mode="clip"))

    mixed, token_grad, landed = rows_plan(
        tokens, out_grad, target, probs, gate_up[0], down[0], relocate
    )
    update_gu, update_down = unpack(
        landed.reshape(-1, landed.shape[2]), first_gu[0], first_down[0]
    )
    return (mixed, token_grad, update_gu[None], update_down[None])


def solution(mesh):
    placed = (
        P(("expert", "dp"), None),
        P(("expert", "dp"), None),
        P(("expert", "dp"), None),
        P(("expert", "dp"), None),
        P(),
        P(),
        P("expert", None, None),
        P("expert", None, None),
        P("expert", "dp", None),
        P("expert", "dp", None),
        P("expert", None, "dp"),
        P("expert", None, "dp"),
    )
    return jax.shard_map(
        per_device,
        mesh=mesh,
        in_specs=placed,
        out_specs=(
            P(("expert", "dp"), None),
            P(("expert", "dp"), None),
            P("expert", "dp", None),
            P("expert", None, "dp"),
        ),
        check_vma=False,
    )
```
